32 devices in a mesh: dp: 8 (over y, x, core), seq: 4 (over z).
Axes of the slice: x: 2, y: 2, z: 4, core: 2. Of those that a mesh axis runs over, the one named last changes fastest.
Arguments:
- queries: bfloat16 [4096, 1280], P(('dp', 'seq')), may hold values from -6 to 6
- key_states: bfloat16 [4096, 1280], P(('dp', 'seq')), may hold values from -6 to 6
- value_states: bfloat16 [4096, 1280], P(('dp', 'seq')), may hold values from -6 to 6
- out_grads: bfloat16 [4096, 1280], P(('dp', 'seq')), may hold values from -6 to 6
- row_order: int32 [4096], P(('dp', 'seq')), may hold values from 0 to 127, as said below
- segment_ids: int32 [8, 512], P('dp'), may hold values from 0 to 1, as said below
Outputs:
- grad_queries: bfloat16 [4096, 1280], P(('dp', 'seq'))
- grad_keys: bfloat16 [4096, 1280], P(('dp', 'seq'))
- grad_values: bfloat16 [4096, 1280], P(('dp', 'seq'))
The draws below stay inside these ranges and needn't reach their ends.
Inputs may be any that keep to these rules, and one draw needn't show every extreme that they name: `row_order`: each block of 128 entries names every number of 0 to 127 once. `segment_ids`: each row holds two screenshots: ids 0 then 1, never falling; the first row with id 1 lies between 192 and 320.
All inputs are finite; a program needn't handle non-finite values.
Results may differ from the reference program's by a relative error of at most 0.012.
Values may be sent and summed in bfloat16 or wider, within the bound.
No kernel may reach another device: no remote copies, remote signals or barrier semaphores. Data moves between devices by JAX's collectives and lax.ppermute only.
A program may use at most 64 MiB of HBM per device.

```python
import math
import jax
import jax.numpy as jnp
from jax import lax

H = 16
HD = 80
D = 1280
TOK_DEV = 128
GROUPS = 8
GROUP_ROWS = 512
SLICE = 16
TOKENS = 4096
N_DP = 8
N_SEQ = 4


def order_table(key):
    device_keys = jax.random.split(jax.random.fold_in(key, 101), TOKENS // TOK_DEV)
    return jax.vmap(lambda device_key: jax.random.permutation(device_key, TOK_DEV))(device_keys).astype(jnp.int32)


def segment_table(key):
    cuts = jax.random.randint(jax.random.fold_in(key, 202), (GROUPS, 1), 3 * GROUP_ROWS // 8, 5 * GROUP_ROWS // 8 + 1)
    positions = jnp.arange(GROUP_ROWS)
    return (positions[None, :] >= cuts).astype(jnp.int32)


def paired_states(key):
    base = jax.random.fold_in(key, 303)
    query_part = jnp.clip(jax.random.normal(jax.random.fold_in(base, 6), (TOKENS, D)), -6.0, 6.0)
    key_part = jnp.clip(jax.random.normal(jax.random.fold_in(base, 7), (TOKENS, D)), -6.0, 6.0)
    return (query_part, key_part)


def draw_queries(key, part):
    return paired_states(key)[0].astype(jnp.bfloat16)


def draw_key_states(key, part):
    return paired_states(key)[1].astype(jnp.bfloat16)


def draw_row_order(key, part):
    return order_table(key).reshape(-1)


def draw_segment_ids(key, part):
    return segment_table(key)


def level_of(key, extent, shards, low, top_value):
    loudness = 1.0
    for position, blocks in shards:
        heights = jax.random.uniform(jax.random.fold_in(jax.random.fold_in(key, 6), position), (blocks,), jnp.float32, low / len(shards), top_value / len(shards))
        loudness = loudness * jnp.repeat(jnp.exp(heights), extent[position] // blocks).reshape((-1,) + (1,) * (len(extent) - 1 - position))
    return loudness


def scatter_about(own_key, dims, deviation, reach, cuts=(), kind=jnp.bfloat16):
    gain = level_of(own_key, dims, cuts, -0.22, 0.18) if cuts else 1.0
    values = jax.random.normal(own_key, dims, jnp.float32) * deviation * gain
    return jnp.minimum(jnp.maximum(values, -reach), reach).astype(kind)


def setup_inputs(seed: int = 0) -> dict:
    key_list = jax.random.split(jax.random.key(seed), 7)
    return {
        "queries": draw_queries(jax.random.fold_in(key_list[6], 71), 0),
        "key_states": draw_key_states(jax.random.fold_in(key_list[6], 71), 0),
        "value_states": scatter_about(key_list[2], (TOKENS, D), 1.0, 6.0, ((0, 32),)),
        "out_grads": scatter_about(key_list[3], (TOKENS, D), 1.0, 6.0, ((0, 32),)),
        "row_order": draw_row_order(jax.random.fold_in(key_list[6], 71), 0),
        "segment_ids": draw_segment_ids(jax.random.fold_in(key_list[6], 71), 0),
    }


def head_grads(head_q, head_k, head_v, head_g, matched, inv_root):
    scores = jnp.dot(head_q, head_k.T, preferred_element_type=jnp.float32) * inv_root
    scores = jnp.where(matched, scores, -1e+30)
    shifted = jnp.exp(scores - lax.optimization_barrier(jnp.max(scores, axis=-1, keepdims=True)))
    probs = shifted / lax.optimization_barrier(jnp.sum(shifted, axis=-1, keepdims=True))
    probs_low = probs.astype(jnp.bfloat16)
    attended = jnp.dot(probs_low, head_v, preferred_element_type=jnp.float32)
    delta = lax.optimization_barrier(jnp.sum(head_g.astype(jnp.float32) * attended, axis=-1, keepdims=True))
    dprobs = jnp.dot(head_g, head_v.T, preferred_element_type=jnp.float32)
    dscores = (probs * (dprobs - delta) * inv_root).astype(jnp.bfloat16)
    grad_q = jnp.dot(dscores, head_k, preferred_element_type=jnp.float32).astype(jnp.bfloat16)
    grad_k = jnp.dot(dscores.T, head_q, preferred_element_type=jnp.float32).astype(jnp.bfloat16)
    grad_v = jnp.dot(probs_low.T, head_g, preferred_element_type=jnp.float32).astype(jnp.bfloat16)
    return (grad_q, grad_k, grad_v)

def group_grads(group_q, group_k, group_v, group_g, group_seg):
    inv_root = 1.0 / math.sqrt(HD)
    matched = group_seg[:, None] == group_seg[None, :]

    def split_heads(array):
        return array.reshape(GROUP_ROWS, H, HD).transpose(1, 0, 2)

    def per_head(items):
        return head_grads(items[0], items[1], items[2], items[3], matched, inv_root)
    results = lax.map(per_head, (split_heads(group_q), split_heads(group_k), split_heads(group_v), split_heads(group_g)))
    return tuple((item.transpose(1, 0, 2).reshape(GROUP_ROWS, D) for item in results))

def reference(queries, key_states, value_states, out_grads, row_order, segment_ids):
    devices = N_DP * N_SEQ
    order_blocks = row_order.reshape(devices, TOK_DEV).astype(jnp.int32)

    def balance(array):
        blocks = array.reshape(devices, TOK_DEV, D)
        permuted = jnp.take_along_axis(blocks, order_blocks[:, :, None], axis=1)
        moved = permuted.reshape(N_DP, N_SEQ, N_DP, SLICE, D).transpose(2, 1, 0, 3, 4)
        return moved.reshape(N_DP, GROUP_ROWS, D)

    def per_group(items):
        return group_grads(items[0], items[1], items[2], items[3], items[4])
    results = lax.map(per_group, (balance(queries), balance(key_states), balance(value_states), balance(out_grads), segment_ids))

    def restore(array):
        moved = array.reshape(N_DP, N_SEQ, N_DP, SLICE, D).transpose(2, 1, 0, 3, 4).reshape(devices, TOK_DEV, D)
        placed = jax.vmap(lambda block, order: jnp.zeros_like(block).at[order].set(block))(moved, order_blocks)
        return placed.reshape(TOKENS, D)
    return (restore(results[0]), restore(results[1]), restore(results[2]))
```

```python
import functools
import math

import jax
import jax.numpy as jnp
from jax import lax
from jax.experimental import pallas as pl
from jax.experimental.pallas import tpu as pltpu
from jax.sharding import PartitionSpec as P

HD = 80
NEG_FILL = -1e30
VMEM_LIMIT = 48 * 1024 * 1024
NT = (((1,), (1,)), ((), ()))
LANES = 128


def in_vmem(count):
    return [pl.BlockSpec(memory_space=pltpu.VMEM)] * count


def params():
    return pltpu.CompilerParams(vmem_limit_bytes=VMEM_LIMIT)


def bf16(*shape):
    return jax.ShapeDtypeStruct(shape, jnp.bfloat16)


def one_hot_columns(order_ref, rows):
    source = lax.broadcasted_iota(jnp.int32, (rows, rows), 0)
    return (source == order_ref[...]).astype(jnp.bfloat16)


def segment_marks(seg_ref, seq_devs, slice_rows):
    rows = seg_ref.shape[1]
    cut = jnp.sum(jnp.where(seg_ref[...] == 0, 1, 0))
    place = lax.broadcasted_iota(jnp.int32, (rows, 2), 0)
    device, part = (place // slice_rows) % seq_devs, place // (slice_rows * seq_devs)
    row = device * (rows // seq_devs) + part * slice_rows + place % slice_rows
    first = jnp.where(row < cut, 1.0, 0.0)
    own = jnp.where(lax.broadcasted_iota(jnp.int32, (rows, 2), 1) == 0, first, 1.0 - first)
    blank = jnp.zeros((rows, LANES - 2), jnp.float32)
    return tuple(
        jnp.concatenate([blank[:, :HD], mark, blank[:, HD:]], axis=1).astype(jnp.bfloat16)
        for mark in (own, (1.0 - own) * NEG_FILL)
    )


def chunk_rows(total):
    step = min(total, 32)
    return [slice(start, start + step) for start in range(0, total, step)]


def eights(chunk, reduce):
    return reduce(chunk.reshape(chunk.shape[0] // 8, 8, chunk.shape[1]), axis=0)


def score_passes(score_ref, dprob_ref, at, probs_ref, dscores_ref):
    scale = math.log2(math.e) / math.sqrt(HD)
    chunks = chunk_rows(score_ref.shape[0])
    top = functools.reduce(jnp.maximum, [eights(score_ref[rows], jnp.max) for rows in chunks])
    top = jnp.max(top, axis=0, keepdims=True) * scale
    total = jnp.zeros((8, score_ref.shape[1]), jnp.float32)
    delta = total
    for rows in chunks:
        shifted = jnp.exp2(score_ref[rows] * scale - top)
        score_ref[rows] = shifted
        total += eights(shifted, jnp.sum)
        delta += eights(shifted * dprob_ref[rows], jnp.sum)
    weight = 1.0 / jnp.sum(total, axis=0, keepdims=True)
    delta = jnp.sum(delta, axis=0, keepdims=True) * weight
    for rows in chunks:
        probs = score_ref[rows] * weight
        probs_ref[rows, at] = probs.astype(jnp.bfloat16)
        dscores_ref[rows, at] = (probs * (dprob_ref[rows] - delta)).astype(jnp.bfloat16)


def pack_kernel(folds, seg_ref, order_ref, *refs):
    inputs, (out_ref, query_mark, key_mark, hot_ref), (landed, seg_vmem, order_vmem, sems) = refs[:4], refs[4:8], refs[8:]
    rows, columns = inputs[0].shape
    seq_devs, slice_rows = out_ref.shape[1:3]
    own = columns // seq_devs
    copies = [
        pltpu.make_async_copy(order_ref, order_vmem, sems.at[4]),
        pltpu.make_async_copy(seg_ref, seg_vmem, sems.at[5]),
    ]
    copies += [pltpu.make_async_copy(ref, landed.at[index], sems.at[index]) for index, ref in enumerate(inputs)]
    for copy in copies:
        copy.start()
    copies[0].wait()
    columns_hot = one_hot_columns(order_vmem, rows)
    hot = columns_hot.T
    if folds > 1:
        places = columns_hot.astype(jnp.float32).T.reshape(rows // slice_rows, folds, slice_rows // folds, rows)
        places = [places[:, fold].reshape(rows // folds, rows) for fold in range(folds)]
        columns_hot = jnp.concatenate(places, axis=0).T.astype(jnp.bfloat16)
    hot_ref[...] = columns_hot
    copies[1].wait()
    query_mark[...], key_mark[...] = segment_marks(seg_vmem, seq_devs, slice_rows)
    for index in range(4):
        copies[2 + index].wait()
        permuted = jnp.dot(hot, landed[index], preferred_element_type=jnp.float32).astype(jnp.bfloat16)
        for peer in range(seq_devs):
            columns_of = permuted[:, peer * own : (peer + 1) * own]
            out_ref[:, peer, :, index * own : (index + 1) * own] = columns_of.reshape(-1, slice_rows, own)


def attention_kernel(heads, folds, slice_rows, query_mark, key_mark, x_ref, out_ref, scores, dprobs, probs, dscores):
    rows, span = scores.shape[1:]
    width, part = 3 * heads * HD, slice_rows // folds
    inv_root = 1.0 / math.sqrt(HD)

    def piece(array, head):
        return x_ref[:, (array * heads + head) * HD : (array * heads + head + 1) * HD]

    def products(step):
        head, at = steps[step]
        if head not in held:
            held[head] = tuple(piece(array, head) for array in range(4))
        query, key, value, grad = held[head]
        marked_query = jnp.concatenate([query[at], query_mark[at, HD:]], axis=1)
        marked_key = jnp.concatenate([key, key_mark[:, HD:]], axis=1)
        scores[step % 2] = lax.dot_general(marked_key, marked_query, NT, preferred_element_type=jnp.float32)
        dprobs[step % 2] = lax.dot_general(value, grad[at], NT, preferred_element_type=jnp.float32)

    def store(array, head, value):
        start = (array * heads + head) * HD
        split = value.reshape(rows // slice_rows, folds, part, HD)
        for fold in range(folds):
            out_ref[:, fold * width + start : fold * width + start + HD] = (
                split[:, fold].reshape(rows // folds, HD).astype(jnp.bfloat16)
            )

    held = {}
    steps = [(head, slice(start, start + span)) for head in range(heads) for start in range(0, rows, span)]
    products(0)
    for step, (head, at) in enumerate(steps):
        if step + 1 < len(steps):
            products(step + 1)
        slot = head % probs.shape[0]
        score_passes(scores.at[step % 2], dprobs.at[step % 2], at, probs.at[slot], dscores.at[slot])
        if at.stop == rows:
            query, key, _, grad = held[head]
            grad_q = jnp.dot(key.T, dscores[slot], preferred_element_type=jnp.float32)
            store(0, head, grad_q.T * inv_root)
            store(1, head, jnp.dot(dscores[slot], query, preferred_element_type=jnp.float32) * inv_root)
            store(2, head, jnp.dot(probs[slot], grad, preferred_element_type=jnp.float32))


def unpack_kernel(folds, hot_ref, packed_ref, *outs):
    rows, columns = outs[0].shape
    seq_devs = packed_ref.shape[1]
    own = columns // seq_devs
    hot = hot_ref[...]
    for index, ref in enumerate(outs):
        whole = []
        for fold in range(folds):
            start = (fold * 3 + index) * own
            pieces = [
                packed_ref[:, peer, :, start : start + own].reshape(rows // folds, own) for peer in range(seq_devs)
            ]
            whole.append(jnp.concatenate(pieces, axis=1))
        ref[...] = jnp.dot(
            hot, jnp.concatenate(whole, axis=0), preferred_element_type=jnp.float32
        ).astype(jnp.bfloat16)


def on_device(queries, key_states, value_states, out_grads, row_order, segment_ids):
    rows, columns = queries.shape
    dp_devs, seq_devs = lax.axis_size("dp"), lax.axis_size("seq")
    own = columns // seq_devs
    heads = own // HD
    peers = dp_devs * seq_devs
    slice_rows = rows // dp_devs
    group_rows = rows * seq_devs
    span = min(group_rows, 512)
    folds = 2 if slice_rows % 16 == 0 and 3 * own % 128 else 1
    order = row_order.reshape(1, rows)
    arrays = (segment_ids, order, queries, key_states, value_states, out_grads)

    packed, query_mark, key_mark, hot = pl.pallas_call(
        functools.partial(pack_kernel, folds),
        out_shape=[
            bf16(dp_devs, seq_devs, slice_rows, 4 * own),
            bf16(group_rows, LANES),
            bf16(group_rows, LANES),
            bf16(rows, rows),
        ],
        in_specs=[pl.BlockSpec(memory_space=pltpu.HBM)] * 6,
        out_specs=in_vmem(4),
        scratch_shapes=[
            pltpu.VMEM((4, rows, columns), jnp.bfloat16),
            pltpu.VMEM((1, group_rows), jnp.int32),
            pltpu.VMEM((1, rows), jnp.int32),
            pltpu.SemaphoreType.DMA((6,)),
        ],
        compiler_params=params(),
        name="pack",
    )(*(pltpu.with_memory_space_constraint(array, pltpu.HBM) for array in arrays))
    moved = lax.all_to_all(
        packed.reshape(peers, slice_rows, 4 * own), ("dp", "seq"), split_axis=0, concat_axis=0, tiled=True
    )
    grads = pl.pallas_call(
        functools.partial(attention_kernel, heads, folds, slice_rows),
        out_shape=bf16(group_rows // folds, folds * 3 * own),
        in_specs=in_vmem(3),
        out_specs=in_vmem(1)[0],
        scratch_shapes=[
            pltpu.VMEM((2, group_rows, span), jnp.float32),
            pltpu.VMEM((2, group_rows, span), jnp.float32),
            pltpu.VMEM((min(heads, 2), group_rows, group_rows), jnp.bfloat16),
            pltpu.VMEM((min(heads, 2), group_rows, group_rows), jnp.bfloat16),
        ],
        compiler_params=params(),
        name="attention",
    )(query_mark, key_mark, moved.reshape(group_rows, 4 * own))
    returned = lax.all_to_all(
        grads.reshape(peers, slice_rows // folds, folds * 3 * own),
        ("dp", "seq"),
        split_axis=0,
        concat_axis=0,
        tiled=True,
    )
    return pl.pallas_call(
        functools.partial(unpack_kernel, folds),
        out_shape=[bf16(rows, columns)] * 3,
        in_specs=in_vmem(2),
        out_specs=in_vmem(3),
        compiler_params=params(),
        name="unpack",
    )(hot, returned.reshape(dp_devs, seq_devs, slice_rows // folds, folds * 3 * own))


def solution(mesh):
    rows = P(("dp", "seq"), None)
    return jax.shard_map(
        on_device,
        mesh=mesh,
        in_specs=(rows, rows, rows, rows, P(("dp", "seq")), P("dp", None)),
        out_specs=(rows, rows, rows),
        check_vma=False,
    )
```

```python
import functools
import math

import jax
import jax.numpy as jnp
from jax import lax
from jax.experimental import pallas as pl
from jax.experimental.pallas import tpu as pltpu
from jax.sharding import PartitionSpec as P

HD = 80
NEG_FILL = -1e30
VMEM_LIMIT = 48 * 1024 * 1024
NT = (((1,), (1,)), ((), ()))
LANES = 128


def in_vmem(count):
    return [pl.BlockSpec(memory_space=pltpu.VMEM)] * count


def params():
    return pltpu.CompilerParams(vmem_limit_bytes=VMEM_LIMIT)


def bf16(*shape):
    return jax.ShapeDtypeStruct(shape, jnp.bfloat16)


def one_hot_columns(order_ref, rows):
    source = lax.broadcasted_iota(jnp.int32, (rows, rows), 0)
    return (source == order_ref[...]).astype(jnp.bfloat16)


def segment_marks(seg_ref, seq_devs, slice_rows):
    rows = seg_ref.shape[1]
    cut = jnp.sum(jnp.where(seg_ref[...] == 0, 1, 0))
    place = lax.broadcasted_iota(jnp.int32, (rows, 2), 0)
    device, part = (place // slice_rows) % seq_devs, place // (slice_rows * seq_devs)
    row = device * (rows // seq_devs) + part * slice_rows + place % slice_rows
    first = jnp.where(row < cut, 1.0, 0.0)
    own = jnp.where(lax.broadcasted_iota(jnp.int32, (rows, 2), 1) == 0, first, 1.0 - first)
    blank = jnp.zeros((rows, LANES - 2), jnp.float32)
    return tuple(
        jnp.concatenate([blank[:, :HD], mark, blank[:, HD:]], axis=1).astype(jnp.bfloat16)
        for mark in (own, (1.0 - own) * NEG_FILL)
    )


def chunk_rows(total):
    step = min(total, 32)
    return [slice(start, start + step) for start in range(0, total, step)]


def eights(chunk, reduce):
    return reduce(chunk.reshape(chunk.shape[0] // 8, 8, chunk.shape[1]), axis=0)


def score_passes(score_ref, dprob_ref, at, probs_ref, dscores_ref):
    scale = math.log2(math.e) / math.sqrt(HD)
    chunks = chunk_rows(score_ref.shape[0])
    top = functools.reduce(jnp.maximum, [eights(score_ref[rows], jnp.max) for rows in chunks])
    top = jnp.max(top, axis=0, keepdims=True) * scale
    total = jnp.zeros((8, score_ref.shape[1]), jnp.float32)
    delta = total
    for rows in chunks:
        shifted = jnp.exp2(score_ref[rows] * scale - top)
        score_ref[rows] = shifted
        total += eights(shifted, jnp.sum)
        delta += eights(shifted * dprob_ref[rows], jnp.sum)
    weight = 1.0 / jnp.sum(total, axis=0, keepdims=True)
    delta = jnp.sum(delta, axis=0, keepdims=True) * weight
    for rows in chunks:
        probs = score_ref[rows] * weight
        probs_ref[rows, at] = probs.astype(jnp.bfloat16)
        dscores_ref[rows, at] = (probs * (dprob_ref[rows] - delta)).astype(jnp.bfloat16)


def pack_kernel(folds, seg_ref, order_ref, *refs):
    inputs, (out_ref, query_mark, key_mark, hot_ref), (landed, seg_vmem, order_vmem, sems) = refs[:4], refs[4:8], refs[8:]
    rows, columns = inputs[0].shape
    seq_devs, slice_rows = out_ref.shape[1:3]
    own = columns // seq_devs
    copies = [
        pltpu.make_async_copy(order_ref, order_vmem, sems.at[4]),
        pltpu.make_async_copy(seg_ref, seg_vmem, sems.at[5]),
    ]
    copies += [pltpu.make_async_copy(ref, landed.at[index], sems.at[index]) for index, ref in enumerate(inputs)]
    for copy in copies:
        copy.start()
    copies[0].wait()
    columns_hot = one_hot_columns(order_vmem, rows)
    hot = columns_hot.T
    if folds > 1:
        places = columns_hot.astype(jnp.float32).T.reshape(rows // slice_rows, folds, slice_rows // folds, rows)
        places = [places[:, fold].reshape(rows // folds, rows) for fold in range(folds)]
        columns_hot = jnp.concatenate(places, axis=0).T.astype(jnp.bfloat16)
    hot_ref[...] = columns_hot
    copies[1].wait()
    query_mark[...], key_mark[...] = segment_marks(seg_vmem, seq_devs, slice_rows)
    for index in range(4):
        copies[2 + index].wait()
        permuted = jnp.dot(hot, landed[index], preferred_element_type=jnp.float32).astype(jnp.bfloat16)
        for peer in range(seq_devs):
            columns_of = permuted[:, peer * own : (peer + 1) * own]
            out_ref[:, peer, :, index * own : (index + 1) * own] = columns_of.reshape(-1, slice_rows, own)


def attention_kernel(heads, folds, slice_rows, query_mark, key_mark, x_ref, out_ref, scores, dprobs, probs, dscores, grad_q):
    rows, span = scores.shape[1:]
    width, part = 3 * heads * HD, slice_rows // folds
    inv_root = 1.0 / math.sqrt(HD)

    def piece(array, head):
        return x_ref[:, (array * heads + head) * HD : (array * heads + head + 1) * HD]

    def products(step):
        head, at = steps[step]
        if head not in held:
            held[head] = tuple(piece(array, head) for array in range(4))
        query, key, value, grad = held[head]
        marked_query = jnp.concatenate([query[at], query_mark[at, HD:]], axis=1)
        marked_key = jnp.concatenate([key, key_mark[:, HD:]], axis=1)
        scores[step % 2] = lax.dot_general(marked_key, marked_query, NT, preferred_element_type=jnp.float32)
        dprobs[step % 2] = lax.dot_general(value, grad[at], NT, preferred_element_type=jnp.float32)

    def store(array, head, value):
        start, columns = (array * heads + head) * HD, value.shape[1]
        split = value.reshape(rows // slice_rows, folds, part, columns)
        for fold in range(folds):
            out_ref[:, fold * width + start : fold * width + start + columns] = (
                split[:, fold].reshape(rows // folds, columns).astype(jnp.bfloat16)
            )

    own = heads * HD
    first = own // LANES * LANES
    key_t = x_ref[:, first : -(-2 * own // LANES) * LANES].T[own - first : 2 * own - first]
    held = {}
    steps = [(head, slice(start, start + span)) for head in range(heads) for start in range(0, rows, span)]
    products(0)
    for step, (head, at) in enumerate(steps):
        if step + 1 < len(steps):
            products(step + 1)
        slot = head % probs.shape[0]
        score_passes(scores.at[step % 2], dprobs.at[step % 2], at, probs.at[slot], dscores.at[slot])
        if at.stop == rows:
            query, _, _, grad = held[head]
            lanes = slice(head * HD, (head + 1) * HD)
            grad_q[lanes, :] = jnp.dot(key_t[lanes], dscores[slot], preferred_element_type=jnp.float32)
            store(1, head, jnp.dot(dscores[slot], query, preferred_element_type=jnp.float32) * inv_root)
            store(2, head, jnp.dot(probs[slot], grad, preferred_element_type=jnp.float32))
    store(0, 0, grad_q[...].T * inv_root)


def unpack_kernel(folds, hot_ref, packed_ref, *outs):
    rows, columns = outs[0].shape
    seq_devs = packed_ref.shape[1]
    own = columns // seq_devs
    hot = hot_ref[...]
    for index, ref in enumerate(outs):
        whole = []
        for fold in range(folds):
            start = (fold * 3 + index) * own
            pieces = [
                packed_ref[:, peer, :, start : start + own].reshape(rows // folds, own) for peer in range(seq_devs)
            ]
            whole.append(jnp.concatenate(pieces, axis=1))
        ref[...] = jnp.dot(
            hot, jnp.concatenate(whole, axis=0), preferred_element_type=jnp.float32
        ).astype(jnp.bfloat16)


def on_device(queries, key_states, value_states, out_grads, row_order, segment_ids):
    rows, columns = queries.shape
    dp_devs, seq_devs = lax.axis_size("dp"), lax.axis_size("seq")
    own = columns // seq_devs
    heads = own // HD
    peers = dp_devs * seq_devs
    slice_rows = rows // dp_devs
    group_rows = rows * seq_devs
    span = min(group_rows, 512)
    folds = 2 if slice_rows % 16 == 0 and 3 * own % 128 else 1
    order = row_order.reshape(1, rows)
    arrays = (segment_ids, order, queries, key_states, value_states, out_grads)

    packed, query_mark, key_mark, hot = pl.pallas_call(
        functools.partial(pack_kernel, folds),
        out_shape=[
            bf16(dp_devs, seq_devs, slice_rows, 4 * own),
            bf16(group_rows, LANES),
            bf16(group_rows, LANES),
            bf16(rows, rows),
        ],
        in_specs=[pl.BlockSpec(memory_space=pltpu.HBM)] * 6,
        out_specs=in_vmem(4),
        scratch_shapes=[
            pltpu.VMEM((4, rows, columns), jnp.bfloat16),
            pltpu.VMEM((1, group_rows), jnp.int32),
            pltpu.VMEM((1, rows), jnp.int32),
            pltpu.SemaphoreType.DMA((6,)),
        ],
        compiler_params=params(),
        name="pack",
    )(*(pltpu.with_memory_space_constraint(array, pltpu.HBM) for array in arrays))
    moved = lax.all_to_all(
        packed.reshape(peers, slice_rows, 4 * own), ("dp", "seq"), split_axis=0, concat_axis=0, tiled=True
    )
    grads = pl.pallas_call(
        functools.partial(attention_kernel, heads, folds, slice_rows),
        out_shape=bf16(group_rows // folds, folds * 3 * own),
        in_specs=in_vmem(3),
        out_specs=in_vmem(1)[0],
        scratch_shapes=[
            pltpu.VMEM((2, group_rows, span), jnp.float32),
            pltpu.VMEM((2, group_rows, span), jnp.float32),
            pltpu.VMEM((min(heads, 2), group_rows, group_rows), jnp.bfloat16),
            pltpu.VMEM((min(heads, 2), group_rows, group_rows), jnp.bfloat16),
            pltpu.VMEM((own, group_rows), jnp.float32),
        ],
        compiler_params=params(),
        name="attention",
    )(query_mark, key_mark, moved.reshape(group_rows, 4 * own))
    returned = lax.all_to_all(
        grads.reshape(peers, slice_rows // folds, folds * 3 * own),
        ("dp", "seq"),
        split_axis=0,
        concat_axis=0,
        tiled=True,
    )
    return pl.pallas_call(
        functools.partial(unpack_kernel, folds),
        out_shape=[bf16(rows, columns)] * 3,
        in_specs=in_vmem(2),
        out_specs=in_vmem(3),
        compiler_params=params(),
        name="unpack",
    )(hot, returned.reshape(dp_devs, seq_devs, slice_rows // folds, folds * 3 * own))


def solution(mesh):
    rows = P(("dp", "seq"), None)
    return jax.shard_map(
        on_device,
        mesh=mesh,
        in_specs=(rows, rows, rows, rows, P(("dp", "seq")), P("dp", None)),
        out_specs=(rows, rows, rows),
        check_vma=False,
    )
```

```python
import functools
import math

import jax
import jax.numpy as jnp
from jax import lax
from jax.experimental import pallas as pl
from jax.experimental.pallas import tpu as pltpu
from jax.sharding import PartitionSpec as P

HD = 80
NEG_FILL = -1e30
VMEM_LIMIT = 48 * 1024 * 1024
NT = (((1,), (1,)), ((), ()))
LANES = 128


def in_vmem(count):
    return [pl.BlockSpec(memory_space=pltpu.VMEM)] * count


def params():
    return pltpu.CompilerParams(vmem_limit_bytes=VMEM_LIMIT)


def bf16(*shape):
    return jax.ShapeDtypeStruct(shape, jnp.bfloat16)


def one_hot_columns(order_ref, rows):
    source = lax.broadcasted_iota(jnp.int32, (rows, rows), 0)
    return (source == order_ref[...]).astype(jnp.bfloat16)


def segment_marks(seg_ref, seq_devs, slice_rows):
    rows = seg_ref.shape[1]
    cut = jnp.sum(jnp.where(seg_ref[...] == 0, 1, 0))
    place = lax.broadcasted_iota(jnp.int32, (rows, 2), 0)
    device, part = (place // slice_rows) % seq_devs, place // (slice_rows * seq_devs)
    row = device * (rows // seq_devs) + part * slice_rows + place % slice_rows
    first = jnp.where(row < cut, 1.0, 0.0)
    own = jnp.where(lax.broadcasted_iota(jnp.int32, (rows, 2), 1) == 0, first, 1.0 - first)
    blank = jnp.zeros((rows, LANES - 2), jnp.float32)
    return tuple(
        jnp.concatenate([blank[:, :HD], mark, blank[:, HD:]], axis=1).astype(jnp.bfloat16)
        for mark in (own, (1.0 - own) * NEG_FILL)
    )


def chunk_rows(total):
    step = min(total, 32)
    return [slice(start, start + step) for start in range(0, total, step)]


def eights(chunk, reduce):
    return reduce(chunk.reshape(chunk.shape[0] // 8, 8, chunk.shape[1]), axis=0)


def score_passes(score_ref, dprob_ref, at, probs_ref, dscores_ref):
    scale = math.log2(math.e) / math.sqrt(HD)
    chunks = chunk_rows(score_ref.shape[0])
    top = functools.reduce(jnp.maximum, [eights(score_ref[rows], jnp.max) for rows in chunks])
    top = jnp.max(top, axis=0, keepdims=True) * scale
    total = jnp.zeros((8, score_ref.shape[1]), jnp.float32)
    delta = total
    for rows in chunks:
        shifted = jnp.exp2(score_ref[rows] * scale - top)
        total += eights(shifted, jnp.sum)
        delta += eights(shifted * dprob_ref[rows], jnp.sum)
    total = jnp.sum(total, axis=0, keepdims=True)
    delta = jnp.sum(delta, axis=0, keepdims=True) / total
    top += jnp.log2(total)
    for rows in chunks:
        probs = jnp.exp2(score_ref[rows] * scale - top)
        probs_ref[rows, at] = probs.astype(jnp.bfloat16)
        dscores_ref[rows, at] = (probs * (dprob_ref[rows] - delta)).astype(jnp.bfloat16)


def pack_kernel(folds, seg_ref, order_ref, *refs):
    inputs, (out_ref, query_mark, key_mark, hot_ref), (landed, seg_vmem, order_vmem, sems) = refs[:4], refs[4:8], refs[8:]
    rows, columns = inputs[0].shape
    seq_devs, slice_rows = out_ref.shape[1:3]
    own = columns // seq_devs
    copies = [
        pltpu.make_async_copy(order_ref, order_vmem, sems.at[4]),
        pltpu.make_async_copy(seg_ref, seg_vmem, sems.at[5]),
    ]
    copies += [pltpu.make_async_copy(ref, landed.at[index], sems.at[index]) for index, ref in enumerate(inputs)]
    for copy in copies:
        copy.start()
    copies[0].wait()
    columns_hot = one_hot_columns(order_vmem, rows)
    hot = columns_hot.T
    if folds > 1:
        places = columns_hot.astype(jnp.float32).T.reshape(rows // slice_rows, folds, slice_rows // folds, rows)
        places = [places[:, fold].reshape(rows // folds, rows) for fold in range(folds)]
        columns_hot = jnp.concatenate(places, axis=0).T.astype(jnp.bfloat16)
    hot_ref[...] = columns_hot
    copies[1].wait()
    query_mark[...], key_mark[...] = segment_marks(seg_vmem, seq_devs, slice_rows)
    for index in range(4):
        copies[2 + index].wait()
        permuted = jnp.dot(hot, landed[index], preferred_element_type=jnp.float32).astype(jnp.bfloat16)
        for peer in range(seq_devs):
            columns_of = permuted[:, peer * own : (peer + 1) * own]
            out_ref[:, peer, :, index * own : (index + 1) * own] = columns_of.reshape(-1, slice_rows, own)


def attention_kernel(heads, folds, slice_rows, query_mark, key_mark, x_ref, out_ref, scores, dprobs, probs, dscores):
    rows, span = scores.shape[1:]
    width, part = 3 * heads * HD, slice_rows // folds
    inv_root = 1.0 / math.sqrt(HD)

    def piece(array, head):
        return x_ref[:, (array * heads + head) * HD : (array * heads + head + 1) * HD]

    def products(step):
        head, at = steps[step]
        if head not in held:
            held[head] = tuple(piece(array, head) for array in range(4))
        query, key, value, grad = held[head]
        marked_query = jnp.concatenate([query[at], query_mark[at, HD:]], axis=1)
        marked_key = jnp.concatenate([key, key_mark[:, HD:]], axis=1)
        scores[step % 2] = lax.dot_general(marked_key, marked_query, NT, preferred_element_type=jnp.float32)
        dprobs[step % 2] = lax.dot_general(value, grad[at], NT, preferred_element_type=jnp.float32)

    def store(array, head, value):
        start = (array * heads + head) * HD
        split = value.reshape(rows // slice_rows, folds, part, HD)
        for fold in range(folds):
            out_ref[:, fold * width + start : fold * width + start + HD] = (
                split[:, fold].reshape(rows // folds, HD).astype(jnp.bfloat16)
            )

    held = {}
    steps = [(head, slice(start, start + span)) for head in range(heads) for start in range(0, rows, span)]
    products(0)
    for step, (head, at) in enumerate(steps):
        if step + 1 < len(steps):
            products(step + 1)
        slot = head % probs.shape[0]
        score_passes(scores.at[step % 2], dprobs.at[step % 2], at, probs.at[slot], dscores.at[slot])
        if at.stop == rows:
            query, key, _, grad = held[head]
            grad_q = jnp.dot(key.T, dscores[slot], preferred_element_type=jnp.float32)
            store(0, head, grad_q.T * inv_root)
            store(1, head, jnp.dot(dscores[slot], query, preferred_element_type=jnp.float32) * inv_root)
            store(2, head, jnp.dot(probs[slot], grad, preferred_element_type=jnp.float32))


def unpack_kernel(folds, hot_ref, packed_ref, *outs):
    rows, columns = outs[0].shape
    seq_devs = packed_ref.shape[1]
    own = columns // seq_devs
    hot = hot_ref[...]
    for index, ref in enumerate(outs):
        whole = []
        for fold in range(folds):
            start = (fold * 3 + index) * own
            pieces = [
                packed_ref[:, peer, :, start : start + own].reshape(rows // folds, own) for peer in range(seq_devs)
            ]
            whole.append(jnp.concatenate(pieces, axis=1))
        ref[...] = jnp.dot(
            hot, jnp.concatenate(whole, axis=0), preferred_element_type=jnp.float32
        ).astype(jnp.bfloat16)


def on_device(queries, key_states, value_states, out_grads, row_order, segment_ids):
    rows, columns = queries.shape
    dp_devs, seq_devs = lax.axis_size("dp"), lax.axis_size("seq")
    own = columns // seq_devs
    heads = own // HD
    peers = dp_devs * seq_devs
    slice_rows = rows // dp_devs
    group_rows = rows * seq_devs
    span = min(group_rows, 512)
    folds = 2 if slice_rows % 16 == 0 and 3 * own % 128 else 1
    order = row_order.reshape(1, rows)
    arrays = (segment_ids, order, queries, key_states, value_states, out_grads)

    packed, query_mark, key_mark, hot = pl.pallas_call(
        functools.partial(pack_kernel, folds),
        out_shape=[
            bf16(dp_devs, seq_devs, slice_rows, 4 * own),
            bf16(group_rows, LANES),
            bf16(group_rows, LANES),
            bf16(rows, rows),
        ],
        in_specs=[pl.BlockSpec(memory_space=pltpu.HBM)] * 6,
        out_specs=in_vmem(4),
        scratch_shapes=[
            pltpu.VMEM((4, rows, columns), jnp.bfloat16),
            pltpu.VMEM((1, group_rows), jnp.int32),
            pltpu.VMEM((1, rows), jnp.int32),
            pltpu.SemaphoreType.DMA((6,)),
        ],
        compiler_params=params(),
        name="pack",
    )(*(pltpu.with_memory_space_constraint(array, pltpu.HBM) for array in arrays))
    moved = lax.all_to_all(
        packed.reshape(peers, slice_rows, 4 * own), ("dp", "seq"), split_axis=0, concat_axis=0, tiled=True
    )
    grads = pl.pallas_call(
        functools.partial(attention_kernel, heads, folds, slice_rows),
        out_shape=bf16(group_rows // folds, folds * 3 * own),
        in_specs=in_vmem(3),
        out_specs=in_vmem(1)[0],
        scratch_shapes=[
            pltpu.VMEM((2, group_rows, span), jnp.float32),
            pltpu.VMEM((2, group_rows, span), jnp.float32),
            pltpu.VMEM((min(heads, 2), group_rows, group_rows), jnp.bfloat16),
            pltpu.VMEM((min(heads, 2), group_rows, group_rows), jnp.bfloat16),
        ],
        compiler_params=params(),
        name="attention",
    )(query_mark, key_mark, moved.reshape(group_rows, 4 * own))
    returned = lax.all_to_all(
        grads.reshape(peers, slice_rows // folds, folds * 3 * own),
        ("dp", "seq"),
        split_axis=0,
        concat_axis=0,
        tiled=True,
    )
    return pl.pallas_call(
        functools.partial(unpack_kernel, folds),
        out_shape=[bf16(rows, columns)] * 3,
        in_specs=in_vmem(2),
        out_specs=in_vmem(3),
        compiler_params=params(),
        name="unpack",
    )(hot, returned.reshape(dp_devs, seq_devs, slice_rows // folds, folds * 3 * own))


def solution(mesh):
    rows = P(("dp", "seq"), None)
    return jax.shard_map(
        on_device,
        mesh=mesh,
        in_specs=(rows, rows, rows, rows, P(("dp", "seq")), P("dp", None)),
        out_specs=(rows, rows, rows),
        check_vma=False,
    )
```

```python
import functools
import math

import jax
import jax.numpy as jnp
from jax import lax
from jax.experimental import pallas as pl
from jax.experimental.pallas import tpu as pltpu
from jax.sharding import PartitionSpec as P

HD = 80
NEG_FILL = -1e30
VMEM_LIMIT = 48 * 1024 * 1024
NT = (((1,), (1,)), ((), ()))
LANES = 128


def in_vmem(count):
    return [pl.BlockSpec(memory_space=pltpu.VMEM)] * count


def params():
    return pltpu.CompilerParams(vmem_limit_bytes=VMEM_LIMIT)


def bf16(*shape):
    return jax.ShapeDtypeStruct(shape, jnp.bfloat16)


def one_hot_columns(order_ref, rows):
    source = lax.broadcasted_iota(jnp.int32, (rows, rows), 0)
    return (source == order_ref[...]).astype(jnp.bfloat16)


def segment_marks(seg_ref):
    rows = seg_ref.shape[1]
    cut = jnp.sum(jnp.where(seg_ref[...] == 0, 1, 0))
    first = jnp.where(lax.broadcasted_iota(jnp.int32, (rows, 2), 0) < cut, 1.0, 0.0)
    own = jnp.where(lax.broadcasted_iota(jnp.int32, (rows, 2), 1) == 0, first, 1.0 - first)
    blank = jnp.zeros((rows, LANES - 2), jnp.float32)
    return tuple(
        jnp.concatenate([blank[:, :HD], mark, blank[:, HD:]], axis=1).astype(jnp.bfloat16)
        for mark in (own, (1.0 - own) * NEG_FILL)
    )


def segment_blocks(rows):
    quarter, low, high = rows // 4, rows * 3 // 8, rows * 5 // 8
    step = min(2 * quarter, 256)
    blocks = [(slice(at, at + step), slice(0, rows)) for at in range(quarter, 3 * quarter, step)]
    return blocks + [(slice(0, quarter), slice(0, high)), (slice(3 * quarter, rows), slice(low, rows))]


def eights(chunk, reduce):
    return reduce(chunk.reshape(chunk.shape[0] // 8, 8, chunk.shape[1]), axis=0)


def score_passes(score_ref, dprob_ref, at, keys, probs_ref, dscores_ref):
    scale = math.log2(math.e) / math.sqrt(HD)
    width = at.stop - at.start
    step = 64 * max(256 // width, 1)
    chunks = [slice(start, min(start + step, keys.stop)) for start in range(keys.start, keys.stop, step)]
    top = functools.reduce(jnp.maximum, [eights(score_ref[rows, at], jnp.max) for rows in chunks])
    top = jnp.max(top, axis=0, keepdims=True) * scale
    total = jnp.zeros((8, width), jnp.float32)
    delta = total
    for rows in chunks:
        shifted = jnp.exp2(score_ref[rows, at] * scale - top)
        score_ref[rows, at] = shifted
        total += eights(shifted, jnp.sum)
        delta += eights(shifted * dprob_ref[rows, at], jnp.sum)
    weight = 1.0 / jnp.sum(total, axis=0, keepdims=True)
    delta = jnp.sum(delta, axis=0, keepdims=True) * weight
    for rows in chunks:
        probs = score_ref[rows, at] * weight
        probs_ref[rows, at] = probs.astype(jnp.bfloat16)
        dscores_ref[rows, at] = (probs * (dprob_ref[rows, at] - delta)).astype(jnp.bfloat16)


def pack_kernel(folds, seg_ref, order_ref, *refs):
    inputs, (out_ref, query_mark, key_mark, hot_ref), (landed, seg_vmem, order_vmem, sems) = refs[:4], refs[4:8], refs[8:]
    rows, columns = inputs[0].shape
    seq_devs, slices = out_ref.shape[:2]
    slice_rows, own = rows // slices, columns // seq_devs
    copies = [
        pltpu.make_async_copy(order_ref, order_vmem, sems.at[4]),
        pltpu.make_async_copy(seg_ref, seg_vmem, sems.at[5]),
    ]
    copies += [pltpu.make_async_copy(ref, landed.at[index], sems.at[index]) for index, ref in enumerate(inputs)]
    for copy in copies:
        copy.start()
    copies[0].wait()
    columns_hot = one_hot_columns(order_vmem, rows)
    hot = columns_hot.T
    if folds > 1:
        places = columns_hot.astype(jnp.float32).T.reshape(rows // slice_rows, folds, slice_rows // folds, rows)
        places = [places[:, fold].reshape(rows // folds, rows) for fold in range(folds)]
        columns_hot = jnp.concatenate(places, axis=0).T.astype(jnp.bfloat16)
    hot_ref[...] = columns_hot
    copies[1].wait()
    query_mark[...], key_mark[...] = segment_marks(seg_vmem)
    for index in range(4):
        copies[2 + index].wait()
        permuted = jnp.dot(hot, landed[index], preferred_element_type=jnp.float32).astype(jnp.bfloat16)
        for peer in range(seq_devs):
            columns_of = permuted[:, peer * own : (peer + 1) * own]
            out_ref[peer, :, :, index * own : (index + 1) * own] = columns_of.reshape(slices, slice_rows, own)


def attention_kernel(
    heads, seq_devs, folds, slice_rows, query_mark, key_mark, x_ref, out_ref, scores, dprobs, probs, dscores
):
    rows = scores.shape[1]
    slices = rows // slice_rows // seq_devs
    width, part = 3 * heads * HD, slice_rows // folds
    inv_root = 1.0 / math.sqrt(HD)
    blocks = segment_blocks(rows)

    def piece(array, head):
        return x_ref[:, (array * heads + head) * HD : (array * heads + head + 1) * HD]

    def products(head):
        held[head] = tuple(piece(array, head) for array in range(4))
        query, key, value, grad = held[head]
        marked_query = jnp.concatenate([query, query_mark[:, HD:]], axis=1)
        marked_key = jnp.concatenate([key, key_mark[:, HD:]], axis=1)
        for at, keys in blocks:
            scores[head % 2, keys, at] = lax.dot_general(
                marked_key[keys], marked_query[at], NT, preferred_element_type=jnp.float32
            )
            dprobs[head % 2, keys, at] = lax.dot_general(
                value[keys], grad[at], NT, preferred_element_type=jnp.float32
            )

    def store(array, head, value):
        start = (array * heads + head) * HD
        for fold in range(folds):
            starts = [
                (device * slices + index) * slice_rows + fold * part
                for index in range(slices)
                for device in range(seq_devs)
            ]
            out_ref[:, fold * width + start : fold * width + start + HD] = jnp.concatenate(
                [value[row : row + part] for row in starts], axis=0
            ).astype(jnp.bfloat16)

    for slot in range(probs.shape[0]):
        for at, keys in blocks:
            for out in (slice(0, keys.start), slice(keys.stop, rows)):
                if out.stop > out.start:
                    zero = jnp.zeros((out.stop - out.start, at.stop - at.start), jnp.bfloat16)
                    probs[slot, out, at] = zero
                    dscores[slot, out, at] = zero
    held = {}
    products(0)
    for head in range(heads):
        if head + 1 < heads:
            products(head + 1)
        slot = head % probs.shape[0]
        for at, keys in blocks:
            score_passes(scores.at[head % 2], dprobs.at[head % 2], at, keys, probs.at[slot], dscores.at[slot])
        query, key, _, grad = held[head]
        grad_q = jnp.dot(key.T, dscores[slot], preferred_element_type=jnp.float32)
        store(0, head, grad_q.T * inv_root)
        store(1, head, jnp.dot(dscores[slot], query, preferred_element_type=jnp.float32) * inv_root)
        store(2, head, jnp.dot(probs[slot], grad, preferred_element_type=jnp.float32))


def unpack_kernel(folds, hot_ref, packed_ref, *outs):
    rows, columns = outs[0].shape
    seq_devs = packed_ref.shape[1]
    own = columns // seq_devs
    hot = hot_ref[...]
    for index, ref in enumerate(outs):
        whole = []
        for fold in range(folds):
            start = (fold * 3 + index) * own
            pieces = [
                packed_ref[:, peer, :, start : start + own].reshape(rows // folds, own) for peer in range(seq_devs)
            ]
            whole.append(jnp.concatenate(pieces, axis=1))
        ref[...] = jnp.dot(
            hot, jnp.concatenate(whole, axis=0), preferred_element_type=jnp.float32
        ).astype(jnp.bfloat16)


def on_device(queries, key_states, value_states, out_grads, row_order, segment_ids):
    rows, columns = queries.shape
    dp_devs, seq_devs = lax.axis_size("dp"), lax.axis_size("seq")
    own = columns // seq_devs
    heads = own // HD
    peers = dp_devs * seq_devs
    slice_rows = rows // dp_devs
    group_rows = rows * seq_devs
    folds = 2 if slice_rows % 16 == 0 and 3 * own % 128 else 1
    order = row_order.reshape(1, rows)
    arrays = (segment_ids, order, queries, key_states, value_states, out_grads)

    packed, query_mark, key_mark, hot = pl.pallas_call(
        functools.partial(pack_kernel, folds),
        out_shape=[
            bf16(seq_devs, dp_devs, slice_rows, 4 * own),
            bf16(group_rows, LANES),
            bf16(group_rows, LANES),
            bf16(rows, rows),
        ],
        in_specs=[pl.BlockSpec(memory_space=pltpu.HBM)] * 6,
        out_specs=in_vmem(4),
        scratch_shapes=[
            pltpu.VMEM((4, rows, columns), jnp.bfloat16),
            pltpu.VMEM((1, group_rows), jnp.int32),
            pltpu.VMEM((1, rows), jnp.int32),
            pltpu.SemaphoreType.DMA((6,)),
        ],
        compiler_params=params(),
        name="pack",
    )(*(pltpu.with_memory_space_constraint(array, pltpu.HBM) for array in arrays))
    moved = lax.all_to_all(
        packed.reshape(peers, slice_rows, 4 * own), ("seq", "dp"), split_axis=0, concat_axis=0, tiled=True
    )
    grads = pl.pallas_call(
        functools.partial(attention_kernel, heads, seq_devs, folds, slice_rows),
        out_shape=bf16(group_rows // folds, folds * 3 * own),
        in_specs=in_vmem(3),
        out_specs=in_vmem(1)[0],
        scratch_shapes=[
            pltpu.VMEM((min(heads, 2), group_rows, group_rows), jnp.float32),
            pltpu.VMEM((min(heads, 2), group_rows, group_rows), jnp.float32),
            pltpu.VMEM((min(heads, 2), group_rows, group_rows), jnp.bfloat16),
            pltpu.VMEM((min(heads, 2), group_rows, group_rows), jnp.bfloat16),
        ],
        compiler_params=params(),
        name="attention",
    )(query_mark, key_mark, moved.reshape(group_rows, 4 * own))
    returned = lax.all_to_all(
        grads.reshape(peers, slice_rows // folds, folds * 3 * own),
        ("dp", "seq"),
        split_axis=0,
        concat_axis=0,
        tiled=True,
    )
    return pl.pallas_call(
        functools.partial(unpack_kernel, folds),
        out_shape=[bf16(rows, columns)] * 3,
        in_specs=in_vmem(2),
        out_specs=in_vmem(3),
        compiler_params=params(),
        name="unpack",
    )(hot, returned.reshape(dp_devs, seq_devs, slice_rows // folds, folds * 3 * own))


def solution(mesh):
    rows = P(("dp", "seq"), None)
    return jax.shard_map(
        on_device,
        mesh=mesh,
        in_specs=(rows, rows, rows, rows, P(("dp", "seq")), P("dp", None)),
        out_specs=(rows, rows, rows),
        check_vma=False,
    )
```

```python
import functools
import math

import jax
import jax.numpy as jnp
from jax import lax
from jax.experimental import pallas as pl
from jax.experimental.pallas import tpu as pltpu
from jax.sharding import PartitionSpec as P

HD = 80
NEG_FILL = -1e30
VMEM_LIMIT = 48 * 1024 * 1024
NT = (((1,), (1,)), ((), ()))
LANES = 128


def in_vmem(count):
    return [pl.BlockSpec(memory_space=pltpu.VMEM)] * count


def params():
    return pltpu.CompilerParams(vmem_limit_bytes=VMEM_LIMIT)


def bf16(*shape):
    return jax.ShapeDtypeStruct(shape, jnp.bfloat16)


def one_hot_columns(order_ref, rows):
    source = lax.broadcasted_iota(jnp.int32, (rows, rows), 0)
    return (source == order_ref[...]).astype(jnp.bfloat16)


def segment_marks(seg_ref):
    rows = seg_ref.shape[1]
    cut = jnp.sum(jnp.where(seg_ref[...] == 0, 1, 0))
    first = jnp.where(lax.broadcasted_iota(jnp.int32, (rows, 2), 0) < cut, 1.0, 0.0)
    own = jnp.where(lax.broadcasted_iota(jnp.int32, (rows, 2), 1) == 0, first, 1.0 - first)
    blank = jnp.zeros((rows, LANES - 2), jnp.float32)
    return tuple(
        jnp.concatenate([blank[:, :HD], mark, blank[:, HD:]], axis=1).astype(jnp.bfloat16)
        for mark in (own, (1.0 - own) * NEG_FILL)
    )


def segment_blocks(rows):
    quarter, low, high = rows // 4, rows * 3 // 8, rows * 5 // 8
    step = min(2 * quarter, 256)
    blocks = [(slice(at, at + step), slice(0, rows)) for at in range(quarter, 3 * quarter, step)]
    return blocks + [(slice(0, quarter), slice(0, high)), (slice(3 * quarter, rows), slice(low, rows))]


def eights(chunk, reduce):
    return reduce(chunk.reshape(chunk.shape[0] // 8, 8, chunk.shape[1]), axis=0)


def score_passes(score_ref, dprob_ref, at, keys, probs_ref, dscores_ref):
    scale = math.log2(math.e) / math.sqrt(HD)
    width = at.stop - at.start
    step = 32 * max(256 // width, 1)
    chunks = [slice(start, min(start + step, keys.stop)) for start in range(keys.start, keys.stop, step)]
    top = functools.reduce(jnp.maximum, [eights(score_ref[rows, at], jnp.max) for rows in chunks])
    top = jnp.max(top, axis=0, keepdims=True) * scale
    total = jnp.zeros((8, width), jnp.float32)
    delta = total
    for rows in chunks:
        shifted = jnp.exp2(score_ref[rows, at] * scale - top)
        score_ref[rows, at] = shifted
        total += eights(shifted, jnp.sum)
        delta += eights(shifted * dprob_ref[rows, at], jnp.sum)
    weight = 1.0 / jnp.sum(total, axis=0, keepdims=True)
    delta = jnp.sum(delta, axis=0, keepdims=True) * weight
    for rows in chunks:
        probs = score_ref[rows, at] * weight
        probs_ref[rows, at] = probs.astype(jnp.bfloat16)
        dscores_ref[rows, at] = (probs * (dprob_ref[rows, at] - delta)).astype(jnp.bfloat16)


def pack_kernel(folds, seg_ref, order_ref, *refs):
    inputs, (out_ref, query_mark, key_mark, hot_ref), (landed, seg_vmem, order_vmem, sems) = refs[:4], refs[4:8], refs[8:]
    rows, columns = inputs[0].shape
    seq_devs, slice_rows = out_ref.shape[1:3]
    own = columns // seq_devs
    copies = [
        pltpu.make_async_copy(order_ref, order_vmem, sems.at[4]),
        pltpu.make_async_copy(seg_ref, seg_vmem, sems.at[5]),
    ]
    copies += [pltpu.make_async_copy(ref, landed.at[index], sems.at[index]) for index, ref in enumerate(inputs)]
    for copy in copies:
        copy.start()
    copies[0].wait()
    columns_hot = one_hot_columns(order_vmem, rows)
    hot = columns_hot.T
    if folds > 1:
        places = columns_hot.astype(jnp.float32).T.reshape(rows // slice_rows, folds, slice_rows // folds, rows)
        places = [places[:, fold].reshape(rows // folds, rows) for fold in range(folds)]
        columns_hot = jnp.concatenate(places, axis=0).T.astype(jnp.bfloat16)
    hot_ref[...] = columns_hot
    copies[1].wait()
    query_mark[...], key_mark[...] = segment_marks(seg_vmem)
    for index in range(4):
        copies[2 + index].wait()
        permuted = jnp.dot(hot, landed[index], preferred_element_type=jnp.float32).astype(jnp.bfloat16)
        for peer in range(seq_devs):
            columns_of = permuted[:, peer * own : (peer + 1) * own]
            out_ref[:, peer, :, index * own : (index + 1) * own] = columns_of.reshape(-1, slice_rows, own)


def attention_kernel(
    heads, seq_devs, folds, slice_rows, query_mark, key_mark, x_ref, out_ref, scores, dprobs, probs, dscores
):
    rows = scores.shape[1]
    slices = rows // slice_rows // seq_devs
    width, part = 3 * heads * HD, slice_rows // folds
    inv_root = 1.0 / math.sqrt(HD)
    blocks = segment_blocks(rows)

    def piece(array, head):
        at = slice((array * heads + head) * HD, (array * heads + head + 1) * HD)
        starts = [(index * seq_devs + device) * slice_rows for device in range(seq_devs) for index in range(slices)]
        return jnp.concatenate([x_ref[start : start + slice_rows, at] for start in starts], axis=0)

    def products(head):
        held[head] = tuple(piece(array, head) for array in range(4))
        query, key, value, grad = held[head]
        marked_query = jnp.concatenate([query, query_mark[:, HD:]], axis=1)
        marked_key = jnp.concatenate([key, key_mark[:, HD:]], axis=1)
        for at, keys in blocks:
            scores[head % 2, keys, at] = lax.dot_general(
                marked_key[keys], marked_query[at], NT, preferred_element_type=jnp.float32
            )
            dprobs[head % 2, keys, at] = lax.dot_general(
                value[keys], grad[at], NT, preferred_element_type=jnp.float32
            )

    def store(array, head, value):
        start = (array * heads + head) * HD
        for fold in range(folds):
            starts = [
                (device * slices + index) * slice_rows + fold * part
                for index in range(slices)
                for device in range(seq_devs)
            ]
            out_ref[:, fold * width + start : fold * width + start + HD] = jnp.concatenate(
                [value[row : row + part] for row in starts], axis=0
            ).astype(jnp.bfloat16)

    for slot in range(probs.shape[0]):
        for at, keys in blocks:
            for out in (slice(0, keys.start), slice(keys.stop, rows)):
                if out.stop > out.start:
                    zero = jnp.zeros((out.stop - out.start, at.stop - at.start), jnp.bfloat16)
                    probs[slot, out, at] = zero
                    dscores[slot, out, at] = zero
    held = {}
    products(0)
    for head in range(heads):
        if head + 1 < heads:
            products(head + 1)
        slot = head % probs.shape[0]
        for at, keys in blocks:
            score_passes(scores.at[head % 2], dprobs.at[head % 2], at, keys, probs.at[slot], dscores.at[slot])
        query, key, _, grad = held[head]
        grad_q = jnp.dot(key.T, dscores[slot], preferred_element_type=jnp.float32)
        store(0, head, grad_q.T * inv_root)
        store(1, head, jnp.dot(dscores[slot], query, preferred_element_type=jnp.float32) * inv_root)
        store(2, head, jnp.dot(probs[slot], grad, preferred_element_type=jnp.float32))


def unpack_kernel(folds, hot_ref, packed_ref, *outs):
    rows, columns = outs[0].shape
    seq_devs = packed_ref.shape[1]
    own = columns // seq_devs
    hot = hot_ref[...]
    for index, ref in enumerate(outs):
        whole = []
        for fold in range(folds):
            start = (fold * 3 + index) * own
            pieces = [
                packed_ref[:, peer, :, start : start + own].reshape(rows // folds, own) for peer in range(seq_devs)
            ]
            whole.append(jnp.concatenate(pieces, axis=1))
        ref[...] = jnp.dot(
            hot, jnp.concatenate(whole, axis=0), preferred_element_type=jnp.float32
        ).astype(jnp.bfloat16)


def on_device(queries, key_states, value_states, out_grads, row_order, segment_ids):
    rows, columns = queries.shape
    dp_devs, seq_devs = lax.axis_size("dp"), lax.axis_size("seq")
    own = columns // seq_devs
    heads = own // HD
    peers = dp_devs * seq_devs
    slice_rows = rows // dp_devs
    group_rows = rows * seq_devs
    folds = 2 if slice_rows % 16 == 0 and 3 * own % 128 else 1
    order = row_order.reshape(1, rows)
    arrays = (segment_ids, order, queries, key_states, value_states, out_grads)

    packed, query_mark, key_mark, hot = pl.pallas_call(
        functools.partial(pack_kernel, folds),
        out_shape=[
            bf16(dp_devs, seq_devs, slice_rows, 4 * own),
            bf16(group_rows, LANES),
            bf16(group_rows, LANES),
            bf16(rows, rows),
        ],
        in_specs=[pl.BlockSpec(memory_space=pltpu.HBM)] * 6,
        out_specs=in_vmem(4),
        scratch_shapes=[
            pltpu.VMEM((4, rows, columns), jnp.bfloat16),
            pltpu.VMEM((1, group_rows), jnp.int32),
            pltpu.VMEM((1, rows), jnp.int32),
            pltpu.SemaphoreType.DMA((6,)),
        ],
        compiler_params=params(),
        name="pack",
    )(*(pltpu.with_memory_space_constraint(array, pltpu.HBM) for array in arrays))
    moved = lax.all_to_all(
        packed.reshape(peers, slice_rows, 4 * own), ("dp", "seq"), split_axis=0, concat_axis=0, tiled=True
    )
    grads = pl.pallas_call(
        functools.partial(attention_kernel, heads, seq_devs, folds, slice_rows),
        out_shape=bf16(group_rows // folds, folds * 3 * own),
        in_specs=in_vmem(3),
        out_specs=in_vmem(1)[0],
        scratch_shapes=[
            pltpu.VMEM((min(heads, 2), group_rows, group_rows), jnp.float32),
            pltpu.VMEM((min(heads, 2), group_rows, group_rows), jnp.float32),
            pltpu.VMEM((min(heads, 2), group_rows, group_rows), jnp.bfloat16),
            pltpu.VMEM((min(heads, 2), group_rows, group_rows), jnp.bfloat16),
        ],
        compiler_params=params(),
        name="attention",
    )(query_mark, key_mark, moved.reshape(group_rows, 4 * own))
    returned = lax.all_to_all(
        grads.reshape(peers, slice_rows // folds, folds * 3 * own),
        ("dp", "seq"),
        split_axis=0,
        concat_axis=0,
        tiled=True,
    )
    return pl.pallas_call(
        functools.partial(unpack_kernel, folds),
        out_shape=[bf16(rows, columns)] * 3,
        in_specs=in_vmem(2),
        out_specs=in_vmem(3),
        compiler_params=params(),
        name="unpack",
    )(hot, returned.reshape(dp_devs, seq_devs, slice_rows // folds, folds * 3 * own))


def solution(mesh):
    rows = P(("dp", "seq"), None)
    return jax.shard_map(
        on_device,
        mesh=mesh,
        in_specs=(rows, rows, rows, rows, P(("dp", "seq")), P("dp", None)),
        out_specs=(rows, rows, rows),
        check_vma=False,
    )
```
